32 devices in a mesh: band: 1, rcol: 4 (over y, core), rrow: 8 (over z, x).
Axes of the slice: x: 2, y: 2, z: 4, core: 2. Of those that a mesh axis runs over, the one named last changes fastest.
Arguments:
- spectra: float32 [6, 2, 1536, 1024], P('band', None, ('rcol', 'rrow')), may hold values from -6 to 6
- valid: int32 [1536, 1024], P(('rcol', 'rrow')), may hold values 0 or 1
Outputs:
- cross: float32 [6, 2, 1536, 1152], P('band', None, 'rcol', 'rrow')
The draws below stay inside these ranges and needn't reach their ends.
All inputs are finite; a program needn't handle non-finite values. No bound on the sum of `valid` on one device may be relied on, other than what follows from the above.
Results may differ from the reference program's by a relative error of at most 0.0035.
Values may be sent and summed in bfloat16 or wider, within the bound.
No kernel may reach another device: no remote copies, remote signals or barrier semaphores. Data moves between devices by JAX's collectives and lax.ppermute only.
A program may use at most 128 MiB of HBM per device.

```python
import jax
import jax.numpy as jnp
from jax import lax

F = 6
B = 48
W = 1024
G = 384
CH = 1536
DIST = 3
N_RCOL = 4
N_RROW = 8


def with_ends(array, key, low, top_value):
    place = [jax.random.randint(jax.random.fold_in(key, axis), (), 0, length) for axis, length in enumerate(array.shape)]
    widest = array.shape.index(max(array.shape))
    neighbour = place[:widest] + [(place[widest] + 1) % array.shape[widest]] + place[widest + 1:]
    return array.at[tuple(place)].set(low).at[tuple(neighbour)].set(top_value)


def level_of(rng, shape, shards, least, high):
    def one(position, parts):
        steps = jax.random.uniform(jax.random.fold_in(jax.random.fold_in(rng, 6), position), (parts,), jnp.float32, least / len(shards), high / len(shards))
        return jnp.repeat(jnp.exp(steps), shape[position] // parts).reshape((-1,) + (1,) * (len(shape) - position - 1))

    loudness = one(*shards[0])
    for cut in shards[1:]:
        loudness = loudness * one(*cut)
    return loudness


def gaussian(rng, dims, width, bound, cuts=(), dtype=jnp.bfloat16):
    values = width * jax.random.normal(rng, dims, jnp.float32)
    if cuts:
        values = values * level_of(rng, dims, cuts, -0.22, 0.18)
    return jnp.clip(values, -bound, bound).astype(dtype)


def setup_inputs(seed: int = 0, part: int = 0) -> dict:
    key_of = jax.random.split(jax.random.key(seed), 3)
    part_splits = jax.random.split(jax.random.fold_in(key_of[2], part), 3)
    spectra = gaussian(part_splits[0], (F, 2, CH, W), 1.0, 6.0, ((2, 32),), jnp.float32)
    valid = with_ends((jax.random.randint(key_of[1], (CH, W), 0, 8) < 7).astype(jnp.int32), jax.random.fold_in(key_of[1], 1), 0, 1)
    return dict(spectra=spectra, valid=valid)


def whiten(spectra, valid):
    power = lax.optimization_barrier(jnp.mean(spectra[:, 0] * spectra[:, 0] + spectra[:, 1] * spectra[:, 1], axis=0))
    amplitude = jnp.sqrt(jnp.maximum(power, 1.0))
    factor = valid.astype(jnp.float32) / amplitude
    return (spectra * factor[None, None]).astype(jnp.bfloat16)

def reference(spectra, valid):
    white = whiten(spectra, valid).astype(jnp.float32)
    groups = white.reshape(F, 2, N_RCOL, G, W)
    blocks = []
    for dist in range(DIST):
        partner = jnp.roll(groups, -dist, axis=2)
        real_part = jnp.einsum('fcgw,fchw->fcgh', groups[:, 0], partner[:, 0]) + jnp.einsum('fcgw,fchw->fcgh', groups[:, 1], partner[:, 1])
        imag_part = jnp.einsum('fcgw,fchw->fcgh', groups[:, 1], partner[:, 0]) - jnp.einsum('fcgw,fchw->fcgh', groups[:, 0], partner[:, 1])
        block = jnp.stack([real_part, imag_part], axis=1) / jnp.float32(W)
        blocks.append(block.reshape(F, 2, N_RCOL, G, N_RROW, 1, B))
    whole = jnp.concatenate(blocks, axis=5)
    return whole.reshape(F, 2, CH, N_RROW * DIST * B)
```

```python
import functools

import jax
import jax.numpy as jnp
from jax import lax
from jax.experimental import pallas as pl
from jax.experimental.pallas import tpu as pltpu
from jax.sharding import PartitionSpec as P

VMEM_BYTES = 40 * 1024 * 1024


def moved_by_xor(value, axis, bits):
    count = lax.axis_size(axis)
    return lax.ppermute(value, axis, [(source, source ^ bits) for source in range(count)])


def moved_by_shift(value, axis, steps):
    count = lax.axis_size(axis)
    return lax.ppermute(value, axis, [(source, (source + steps) % count) for source in range(count)])


def whiten_kernel(half_ref, spectra_ref, valid_ref, *out_refs):
    bins = spectra_ref.shape[0]
    share = bins // 2
    half = half_ref[0]
    total = spectra_ref[0, 0] * spectra_ref[0, 0] + spectra_ref[0, 1] * spectra_ref[0, 1]
    for f in range(1, bins):
        total = total + (spectra_ref[f, 0] * spectra_ref[f, 0] + spectra_ref[f, 1] * spectra_ref[f, 1])
    amplitude = jnp.sqrt(jnp.maximum(total / bins, 1.0))
    factor = valid_ref[...].astype(jnp.float32) / amplitude
    for k in range(share):
        for part in range(2):
            kept = spectra_ref[half * share + k, part] * factor
            sent = spectra_ref[(1 - half) * share + k, part] * factor
            out_refs[k][part] = kept.astype(jnp.bfloat16)
            out_refs[share + k][part] = sent.astype(jnp.bfloat16)


def whiten(half, spectra, valid):
    bins, _, channels, windows = spectra.shape
    tile = 16 if channels % 16 == 0 else channels
    white = jax.ShapeDtypeStruct((2, channels, windows), jnp.bfloat16)
    return pl.pallas_call(
        whiten_kernel,
        grid_spec=pltpu.PrefetchScalarGridSpec(
            num_scalar_prefetch=1,
            grid=(channels // tile,),
            in_specs=[
                pl.BlockSpec((bins, 2, tile, windows), lambda i, h: (0, 0, i, 0)),
                pl.BlockSpec((tile, windows), lambda i, h: (i, 0)),
            ],
            out_specs=[pl.BlockSpec((2, tile, windows), lambda i, h: (0, i, 0))] * bins,
        ),
        out_shape=[white] * bins,
        compiler_params=pltpu.CompilerParams(vmem_limit_bytes=VMEM_BYTES),
        name="whiten",
    )(half, spectra, valid)


def times(left, right):
    return lax.dot_general(left, right, (((1,), (1,)), ((), ())), preferred_element_type=jnp.float32)


def cross_kernel(pieces, reach, with_out, bin_ref, place_ref, *refs):
    rows = refs[:pieces]
    near = refs[pieces:pieces + reach]
    far = refs[pieces + reach:pieces + 2 * reach]
    out_ref, sent_ref = refs[-2:]
    height = rows[0].shape[1]
    scale = 1.0 / rows[0].shape[2]
    place = place_ref[0]
    left = jnp.concatenate(
        [jnp.concatenate([ref[0] for ref in rows], axis=0), jnp.concatenate([ref[1] for ref in rows], axis=0)], axis=1
    )

    def columns(refs):
        real = jnp.concatenate([ref[0] for ref in refs], axis=0)
        imag = jnp.concatenate([ref[1] for ref in refs], axis=0)
        return jnp.concatenate([real, imag], axis=1), jnp.concatenate([-imag, real], axis=1)

    for part, right in enumerate(columns(far)):
        sent_ref[part] = (times(right, left) * scale).astype(sent_ref.dtype)
    for part, right in enumerate(columns(near)):
        block = times(left, right) * scale
        for label in range(pieces):
            start = pl.multiple_of((place ^ label) * height, 8)
            out_ref[0, part, pl.ds(start, height), :] = block[label * height:(label + 1) * height]


def cross(bin_index, place, rows, near, far, out, bins):
    pieces, reach = len(rows), len(near)
    _, height, windows = rows[0].shape
    group, width = pieces * height, reach * height
    operands = [*rows, *near, *far]
    specs = [pl.BlockSpec(op.shape, lambda i, b, p: (0, 0, 0)) for op in operands]
    aliases = {}
    if out is not None:
        aliases = {2 + len(operands): 0}
        operands.append(out)
        specs.append(pl.BlockSpec(memory_space=pl.ANY))
    flops = 2 * 8 * group * width * windows
    return pl.pallas_call(
        functools.partial(cross_kernel, pieces, reach, out is not None),
        grid_spec=pltpu.PrefetchScalarGridSpec(
            num_scalar_prefetch=2,
            grid=(1,),
            in_specs=specs,
            out_specs=[
                pl.BlockSpec((1, 2, group, width), lambda i, b, p: (b[0], 0, 0, 0)),
                pl.BlockSpec((2, width, group), lambda i, b, p: (0, 0, 0)),
            ],
        ),
        out_shape=[
            jax.ShapeDtypeStruct((bins, 2, group, width), jnp.float32),
            jax.ShapeDtypeStruct((2, width, group), jnp.bfloat16),
        ],
        input_output_aliases=aliases,
        compiler_params=pltpu.CompilerParams(vmem_limit_bytes=VMEM_BYTES),
        cost_estimate=pl.CostEstimate(flops=flops, bytes_accessed=5_000_000, transcendentals=0),
        name="cross",
    )(bin_index, place, *operands)


def place_kernel(pieces, bin_ref, place_ref, came_ref, _, out_ref):
    height = out_ref.shape[2] // pieces
    place = place_ref[0]
    for part in range(2):
        block = came_ref[part].astype(jnp.float32).T
        for label in range(pieces):
            start = pl.multiple_of((place ^ label) * height, 8)
            out_ref[0, part, pl.ds(start, height), :] = block[label * height:(label + 1) * height]


def place_block(bin_index, place, came, out, pieces):
    _, _, group, width = out.shape
    return pl.pallas_call(
        functools.partial(place_kernel, pieces),
        grid_spec=pltpu.PrefetchScalarGridSpec(
            num_scalar_prefetch=2,
            grid=(1,),
            in_specs=[
                pl.BlockSpec((2, width, group), lambda i, b, p: (0, 0, 0)),
                pl.BlockSpec(memory_space=pl.ANY),
            ],
            out_specs=pl.BlockSpec((1, 2, group, width), lambda i, b, p: (b[0], 0, 0, 0)),
        ),
        out_shape=jax.ShapeDtypeStruct(out.shape, jnp.float32),
        input_output_aliases={3: 0},
        compiler_params=pltpu.CompilerParams(vmem_limit_bytes=VMEM_BYTES),
        name="place",
    )(bin_index, place, came, out)


def shards(spectra, valid):
    bins, _, channels, windows = spectra.shape
    share = bins // 2
    count = lax.axis_size("rrow")
    reach = lax.axis_size("rcol") // 2 + 1
    top = count // 2
    me = lax.axis_index("rrow").astype(jnp.int32)
    half = me // top
    white = whiten(half[None], spectra, valid)
    own, other = white[:share], white[share:]
    arrived = [moved_by_xor(piece, "rrow", top) for piece in other]
    out, returned = None, []
    for k in range(share):
        held = {0: own[k], top: arrived[k]}
        bit = top // 2
        while bit:
            for label, piece in list(held.items()):
                held[label ^ bit] = moved_by_xor(piece, "rrow", bit)
            bit //= 2
        near = [own[k]] + [moved_by_shift(own[k], "rcol", -d) for d in range(1, reach)]
        far = [arrived[k]] + [moved_by_shift(arrived[k], "rcol", -d) for d in range(1, reach)]
        rows = [held[label] for label in range(count)]
        out, sent = cross((half * share + k)[None], me[None], rows, near, far, out, bins)
        returned.append(moved_by_xor(sent, "rrow", top))
    for k in range(share):
        out = place_block(((1 - half) * share + k)[None], (me ^ top)[None], returned[k], out, count)
    return out


def solution(mesh):
    in_specs = (P("band", None, ("rcol", "rrow"), None), P(("rcol", "rrow"), None))
    out_specs = P("band", None, "rcol", "rrow")
    return jax.shard_map(shards, mesh=mesh, in_specs=in_specs, out_specs=out_specs, check_vma=False)
```

```python
import functools

import jax
import jax.numpy as jnp
from jax import lax
from jax.experimental import pallas as pl
from jax.experimental.pallas import tpu as pltpu
from jax.sharding import PartitionSpec as P

COVER = 1
VMEM_BYTES = 64 * 1024 * 1024 - 65536


def moved_by_xor(value, axis, bits):
    count = lax.axis_size(axis)
    return lax.ppermute(value, axis, [(source, source ^ bits) for source in range(count)])


def moved_by_shift(value, axis, steps):
    count = lax.axis_size(axis)
    return lax.ppermute(value, axis, [(source, (source + steps) % count) for source in range(count)])


def after(value, *earlier):
    return lax.optimization_barrier((value, *earlier))[0]


def fence_kernel(token_ref, out_ref):
    out_ref[0] = token_ref[0] + 1


def fence(token, *earlier):
    return pl.pallas_call(
        fence_kernel,
        in_specs=[pl.BlockSpec(memory_space=pltpu.SMEM)],
        out_specs=pl.BlockSpec(memory_space=pltpu.SMEM),
        out_shape=jax.ShapeDtypeStruct((1,), jnp.int32),
        cost_estimate=pl.CostEstimate(flops=COVER, bytes_accessed=1, transcendentals=0),
        name="fence",
    )(after(token, *earlier))


def whiten_kernel(splits, place_ref, spectra_ref, valid_ref, all_ref, front_ref, back_ref, front_other, back_other):
    bins = spectra_ref.shape[0]
    total = spectra_ref[0, 0] * spectra_ref[0, 0] + spectra_ref[0, 1] * spectra_ref[0, 1]
    for f in range(1, bins):
        total = total + (spectra_ref[f, 0] * spectra_ref[f, 0] + spectra_ref[f, 1] * spectra_ref[f, 1])
    amplitude = jnp.sqrt(jnp.maximum(total / bins, 1.0))
    factor = valid_ref[...].astype(jnp.float32) / amplitude
    for k, split in enumerate(splits):
        side = (place_ref[0] // split) % 2
        for part in range(2):
            kept = (spectra_ref[2 * k + side, part] * factor).astype(jnp.bfloat16)
            sent = (spectra_ref[2 * k + 1 - side, part] * factor).astype(jnp.bfloat16)
            all_ref[k, part] = kept
            if k < len(splits) - 1:
                front_ref[k, part] = kept
                front_other[k, part] = sent
            else:
                back_ref[0, part] = kept
                back_other[0, part] = sent


def whiten(splits, place, spectra, valid):
    bins, _, channels, windows = spectra.shape
    tile = windows // 2 if windows % 256 == 0 else windows
    count = len(splits)
    sizes = [count, count - 1, 1, count - 1, 1]
    return pl.pallas_call(
        functools.partial(whiten_kernel, splits),
        grid_spec=pltpu.PrefetchScalarGridSpec(
            num_scalar_prefetch=1,
            grid=(windows // tile,),
            in_specs=[
                pl.BlockSpec((bins, 2, channels, tile), lambda i, p: (0, 0, 0, i)),
                pl.BlockSpec((channels, tile), lambda i, p: (0, i)),
            ],
            out_specs=[pl.BlockSpec((n, 2, channels, tile), lambda i, p: (0, 0, 0, i)) for n in sizes],
        ),
        out_shape=[jax.ShapeDtypeStruct((n, 2, channels, windows), jnp.bfloat16) for n in sizes],
        compiler_params=pltpu.CompilerParams(vmem_limit_bytes=VMEM_BYTES),
        cost_estimate=pl.CostEstimate(flops=1, bytes_accessed=1, transcendentals=0),
        name="whiten",
    )(place, spectra, valid)


def cross_kernel(pieces, reach, slots, before, scalars, *refs):
    slabs = [ref.at[slot] for ref, slot in zip(refs, slots)]
    rows, near, far = slabs[:pieces], slabs[pieces:pieces + reach], slabs[pieces + reach:pieces + 2 * reach]
    out_ref, sent_ref, left_ref, real_ref, imag_ref, mine_ref, theirs_ref, old_ref, new_ref, sems = refs[-10:]
    _, height, windows = rows[0].shape
    width = reach * height
    place, mine_bin, old_bin = scalars[0], scalars[1], scalars[2]
    moves = []

    def move(source, target):
        copy = pltpu.make_async_copy(source, target, sems.at[len(moves)])
        copy.start()
        moves.append(copy)
        return copy

    for side, group in enumerate((near, far)):
        for d, ref in enumerate(group):
            at = pl.ds(side * width + d * height, height)
            move(ref.at[0], real_ref.at[at])
            move(ref.at[1], imag_ref.at[at])
    for label, ref in enumerate(rows):
        start = pl.multiple_of((place ^ label) * height, 16)
        for part in range(2):
            move(ref.at[part], left_ref.at[part, pl.ds(start, height)])
    arriving = list(moves)
    if before:
        came = move(refs[pieces + 2 * reach], old_ref)
        came.wait()
        new_ref[...] = old_ref[...].astype(jnp.float32)
        placed = move(new_ref, out_ref.at[old_bin])
    for copy in arriving:
        copy.wait()

    def times(right, left):
        return lax.dot_general(right, left, (((1,), (1,)), ((), ())), preferred_element_type=jnp.float32)

    real, imag, rows_real, rows_imag = real_ref[...], imag_ref[...], left_ref[0], left_ref[1]
    scale = 1.0 / windows
    for part in range(2):
        if part == 0:
            sums = times(real, rows_real) + times(imag, rows_imag)
        else:
            sums = times(real, rows_imag) - times(imag, rows_real)
        sums = sums * scale
        mine_ref[part] = sums[:width]
        theirs_ref[part] = sums[width:].astype(theirs_ref.dtype)
    ending = [move(theirs_ref, sent_ref), move(mine_ref, out_ref.at[mine_bin])]
    if before:
        ending.append(placed)
    for copy in ending:
        copy.wait()


def cross(scalars, rows, near, far, came, out, bins):
    pieces, reach = len(rows), len(near)
    *_, height, windows = rows[0][0].shape
    group, width = pieces * height, reach * height
    operands = [array for array, _ in (*rows, *near, *far)]
    slots = [slot for _, slot in (*rows, *near, *far)]
    aliases = {}
    if came is not None:
        operands.append(came)
    if out is not None:
        operands.append(out)
        aliases = {len(operands): 0}
    return pl.pallas_call(
        functools.partial(cross_kernel, pieces, reach, slots, came is not None),
        grid_spec=pltpu.PrefetchScalarGridSpec(
            num_scalar_prefetch=1,
            grid=(1,),
            in_specs=[pl.BlockSpec(memory_space=pl.ANY)] * len(operands),
            out_specs=[pl.BlockSpec(memory_space=pl.ANY)] * 2,
            scratch_shapes=[
                pltpu.VMEM((2, group, windows), jnp.bfloat16),
                pltpu.VMEM((2 * width, windows), jnp.bfloat16),
                pltpu.VMEM((2 * width, windows), jnp.bfloat16),
                pltpu.VMEM((2, width, group), jnp.float32),
                pltpu.VMEM((2, width, group), jnp.bfloat16),
                pltpu.VMEM((2, width, group), jnp.bfloat16),
                pltpu.VMEM((2, width, group), jnp.float32),
                pltpu.SemaphoreType.DMA((2 * (pieces + 2 * reach) + 4,)),
            ],
        ),
        out_shape=[
            jax.ShapeDtypeStruct((bins, 2, width, group), jnp.float32),
            jax.ShapeDtypeStruct((2, width, group), jnp.bfloat16),
        ],
        input_output_aliases=aliases,
        compiler_params=pltpu.CompilerParams(vmem_limit_bytes=VMEM_BYTES),
        cost_estimate=pl.CostEstimate(flops=COVER, bytes_accessed=1, transcendentals=0),
        name="cross",
    )(scalars, *operands)


def place_kernel(bin_ref, came_ref, _, out_ref):
    out_ref[0] = came_ref[...].astype(jnp.float32)


def place_block(bin_index, came, out):
    return pl.pallas_call(
        place_kernel,
        grid_spec=pltpu.PrefetchScalarGridSpec(
            num_scalar_prefetch=1,
            grid=(1,),
            in_specs=[
                pl.BlockSpec(came.shape, lambda i, b: (0, 0, 0)),
                pl.BlockSpec(memory_space=pl.ANY),
            ],
            out_specs=pl.BlockSpec((1, *out.shape[1:]), lambda i, b: (b[0], 0, 0, 0)),
        ),
        out_shape=jax.ShapeDtypeStruct(out.shape, jnp.float32),
        input_output_aliases={2: 0},
        compiler_params=pltpu.CompilerParams(vmem_limit_bytes=VMEM_BYTES),
        name="place",
    )(bin_index, came, out)


def shards(spectra, valid):
    bins = spectra.shape[0]
    reach = lax.axis_size("rcol") // 2 + 1
    count = lax.axis_size("rrow")
    me = lax.axis_index("rrow").astype(jnp.int32)
    splits = (4, 4, 2)

    def flip(value, bits, *gates):
        return moved_by_xor(after(value, *gates) if gates else value, "rrow", bits)

    def shift(value, d, *gates):
        return moved_by_shift(after(value, *gates) if gates else value, "rcol", -d)

    def bin_of(k, side):
        return 2 * k + (me // splits[k] + side) % 2

    def rows_of(k, slot, mine_z, mine_d, got, got_x, got_z, got_d):
        split = splits[k]
        other = 6 - split
        held = {
            0: (own, k), 1: (own_x, k), other: (mine_z, slot), other | 1: (mine_d, slot),
            split: (got, slot), split | 1: (got_x, slot), split | other: (got_z, slot), split | other | 1: (got_d, slot),
        }
        return [held[label] for label in range(count)]

    def scalars(k, old):
        return jnp.stack([me, bin_of(k, 0), bin_of(old, 1)])

    own, front, back, front_other, back_other = whiten(splits, me[None], spectra, valid)
    steps = range(1, reach)
    got = flip(front_other, 4)
    own_x = flip(own, 1)
    front_z = flip(front, 2)
    own_y = [own] + [shift(own, d) for d in steps]
    front_d = flip(front_z, 1)
    last = flip(back_other, 2, front_z)
    back_z = flip(back, 4, got)
    got_z = flip(got, 2, last)
    got_x = flip(got, 1, own_x)
    got_y = [got] + [shift(got, d, own_y[d]) for d in steps]
    got_d = flip(got_z, 1, front_d)
    last_z = flip(last, 4, back_z)
    back_d = flip(back_z, 1, got_x)
    last_x = flip(last, 1, got_d)
    last_y = [last] + [shift(last, d, got_y[d]) for d in steps]

    out, sent, came = None, None, []
    for k in range(2):
        rows = rows_of(k, k, front_z, front_d, got, got_x, got_z, got_d)
        near, far = [(x, k) for x in own_y], [(x, k) for x in got_y]
        out, sent = cross(scalars(k, 0), rows, near, far, None, out, bins)
        came.append(flip(sent, 4))
    last_d = flip(last_z, 1, back_d)
    rows = rows_of(2, 0, back_z, back_d, last, last_x, last_z, last_d)
    out, sent = cross(scalars(2, 0), rows, [(x, 2) for x in own_y], [(x, 0) for x in last_y], None, out, bins)
    came.append(flip(sent, 2))
    for k in range(3):
        out = place_block(bin_of(k, 1)[None], after(came[k], sent), out)
    return jnp.swapaxes(out, 2, 3)


def solution(mesh):
    in_specs = (P("band", None, ("rcol", "rrow"), None), P(("rcol", "rrow"), None))
    out_specs = P("band", None, "rcol", "rrow")
    return jax.shard_map(shards, mesh=mesh, in_specs=in_specs, out_specs=out_specs, check_vma=False)
```

```python
import functools

import jax
import jax.numpy as jnp
from jax import lax
from jax.experimental import pallas as pl
from jax.experimental.pallas import tpu as pltpu
from jax.sharding import PartitionSpec as P

VMEM_BYTES = 64 * 1024 * 1024 - 65536


def moved_by_xor(value, axis, bits):
    count = lax.axis_size(axis)
    return lax.ppermute(value, axis, [(source, source ^ bits) for source in range(count)])


def moved_by_shift(value, axis, steps):
    count = lax.axis_size(axis)
    return lax.ppermute(value, axis, [(source, (source + steps) % count) for source in range(count)])


SPLITS = (4, 4, 2)
WHITE = {
    "own": ((0, 0), (1, 0), (2, 0)),
    "front": ((0, 0), (1, 0)),
    "back": ((2, 0),),
    "front_other": ((0, 1), (1, 1)),
    "back_other": ((2, 1),),
}
SENT = {
    "got": ("front_other", "rrow", 4),
    "own_x": ("own", "rrow", 1),
    "front_z": ("front", "rrow", 2),
    "own_y1": ("own", "rcol", 1),
    "own_y2": ("own", "rcol", 2),
    "front_d": ("front_z", "rrow", 1),
    "last": ("back_other", "rrow", 2),
    "back_z": ("back", "rrow", 4),
    "got_z": ("got", "rrow", 2),
    "got_x": ("got", "rrow", 1),
    "got_y1": ("got", "rcol", 1),
    "got_y2": ("got", "rcol", 2),
    "got_d": ("got_z", "rrow", 1),
    "last_z": ("last", "rrow", 4),
    "back_d": ("back_z", "rrow", 1),
    "last_x": ("last", "rrow", 1),
    "last_y1": ("last", "rcol", 1),
    "last_y2": ("last", "rcol", 2),
    "last_d": ("last_z", "rrow", 1),
    "came0": ("far0", "came", 4),
    "came1": ("far1", "came", 4),
    "came2": ("far2", "came", 2),
}
TAKEN = {}
ROWS = {
    0: [("own", 0), ("own_x", 0), ("front_z", 0), ("front_d", 0), ("got", 0), ("got_x", 0), ("got_z", 0), ("got_d", 0)],
    1: [("own", 1), ("own_x", 1), ("front_z", 1), ("front_d", 1), ("got", 1), ("got_x", 1), ("got_z", 1), ("got_d", 1)],
    2: [("own", 2), ("own_x", 2), ("last", 0), ("last_x", 0), ("back_z", 0), ("back_d", 0), ("last_z", 0), ("last_d", 0)],
}
COLUMNS = {
    0: (("own", 0), ("got", 0)),
    1: (("own", 1), ("got", 1)),
    2: (("own", 2), ("last", 0)),
}
FAR = 2
ORDER = ("got", "own_x", "front_z", "own_y1", "own_y2", "front_d", "last", "back_z", "got_z", "got_x", "got_y1", "got_y2", "got_d", "last_z", "back_d", "last_x", "last_y1", "last_y2", "last_d", "far0", "came0", "far1", "came1", "far2", "came2", "near012", "place01", "place2")
GATES = {
    "last": ["front_z"],
    "back_z": ["got"],
    "got_z": ["last"],
    "got_x": ["own_x"],
    "got_y1": ["own_y1"],
    "got_y2": ["own_y2"],
    "got_d": ["front_d"],
    "last_z": ["back_z"],
    "back_d": ["got_x"],
    "last_x": ["got_d"],
    "last_y1": ["got_y1"],
    "last_y2": ["got_y2"],
    "last_d": ["back_d"],
}


def bin_of(place, pair, split, other):
    return 2 * pair + ((place // split) % 2 + other) % 2


def whiten_kernel(plan, splits, place_ref, spectra_ref, valid_ref, *out_refs):
    bins = spectra_ref.shape[0]
    total = spectra_ref[0, 0] * spectra_ref[0, 0] + spectra_ref[0, 1] * spectra_ref[0, 1]
    for f in range(1, bins):
        total = total + (spectra_ref[f, 0] * spectra_ref[f, 0] + spectra_ref[f, 1] * spectra_ref[f, 1])
    amplitude = jnp.sqrt(jnp.maximum(total / bins, 1.0))
    factor = valid_ref[...].astype(jnp.float32) / amplitude
    place = place_ref[0]
    for pair, split in enumerate(splits):
        for other in range(2):
            for part in range(2):
                value = (spectra_ref[bin_of(place, pair, split, other), part] * factor).astype(jnp.bfloat16)
                for out_ref, slabs in zip(out_refs, plan):
                    if (pair, other) in slabs:
                        out_ref[slabs.index((pair, other)), part] = value


def whiten(plan, splits, place, spectra, valid):
    bins, _, channels, windows = spectra.shape
    tile = windows // 2 if windows % 256 == 0 else windows
    return pl.pallas_call(
        functools.partial(whiten_kernel, plan, splits),
        grid_spec=pltpu.PrefetchScalarGridSpec(
            num_scalar_prefetch=1,
            grid=(windows // tile,),
            in_specs=[
                pl.BlockSpec((bins, 2, channels, tile), lambda i, p: (0, 0, 0, i)),
                pl.BlockSpec((channels, tile), lambda i, p: (0, i)),
            ],
            out_specs=[pl.BlockSpec((len(slabs), 2, channels, tile), lambda i, p: (0, 0, 0, i)) for slabs in plan],
        ),
        out_shape=[jax.ShapeDtypeStruct((len(slabs), 2, channels, windows), jnp.bfloat16) for slabs in plan],
        compiler_params=pltpu.CompilerParams(vmem_limit_bytes=VMEM_BYTES),
        cost_estimate=pl.CostEstimate(flops=1, bytes_accessed=1, transcendentals=0),
        name="whiten",
    )(place, spectra, valid)


def cross_kernel(jobs, place_ref, *refs):
    left_ref, right_ref, mine_ref, theirs_ref, sems = refs[-5:]
    out_ref = refs[-6]
    place = place_ref[0]
    height, windows = refs[0].shape[2:]
    moves, started = [], []

    def move(source, target):
        copy = pltpu.make_async_copy(source, target, sems.at[len(started)])
        copy.start()
        started.append(copy)
        return copy

    given = iter(refs)
    for n, (_, _, kind, row_slots, column_slots) in enumerate(jobs):
        arriving = []
        for label, slot in enumerate(row_slots):
            start = pl.multiple_of((place ^ label) * height, 16)
            arriving.append(move(next(given).at[slot], left_ref.at[n, :, pl.ds(start, height)]))
        for d, slot in enumerate(column_slots):
            arriving.append(move(next(given).at[slot], right_ref.at[n, :, pl.ds(d * height, height)]))
        moves.append(arriving)

    scale = 1.0 / windows
    leaving = []
    for n, (pair, split, kind, _, _) in enumerate(jobs):
        for copy in moves[n]:
            copy.wait()
        group, width = left_ref.shape[2], right_ref.shape[2]
        right = right_ref[n].reshape(2 * width, windows)
        left = left_ref[n].reshape(2 * group, windows)
        sums = scale * lax.dot_general(right, left, (((1,), (1,)), ((), ())), preferred_element_type=jnp.float32)
        block_ref = mine_ref if kind == "near" else theirs_ref
        block_ref[n, 0] = (sums[:width, :group] + sums[width:, group:]).astype(block_ref.dtype)
        block_ref[n, 1] = (sums[:width, group:] - sums[width:, :group]).astype(block_ref.dtype)
        target = out_ref.at[bin_of(place, pair, split, 0)] if kind == "near" else out_ref
        leaving.append(move(block_ref.at[n], target))
    for copy in leaving:
        copy.wait()


def cross(place, kind, jobs, out, bins):
    count = len(jobs)
    operands = [array for _, _, rows, columns in jobs for array, _ in (*rows, *columns)]
    plan = [
        (pair, split, kind, tuple(slot for _, slot in rows), tuple(slot for _, slot in columns))
        for pair, split, rows, columns in jobs
    ]
    _, _, rows, columns = jobs[0]
    *_, height, windows = operands[0].shape
    group, width = len(rows) * height, len(columns) * height
    aliases = {}
    if out is not None:
        operands.append(out)
        aliases = {len(operands): 0}
    shape = jax.ShapeDtypeStruct((2, width, group), jnp.bfloat16)
    if kind == "near":
        shape = jax.ShapeDtypeStruct((bins, 2, width, group), jnp.float32)
    return pl.pallas_call(
        functools.partial(cross_kernel, plan),
        grid_spec=pltpu.PrefetchScalarGridSpec(
            num_scalar_prefetch=1,
            grid=(1,),
            in_specs=[pl.BlockSpec(memory_space=pl.ANY)] * len(operands),
            out_specs=pl.BlockSpec(memory_space=pl.ANY),
            scratch_shapes=[
                pltpu.VMEM((count, 2, group, windows), jnp.bfloat16),
                pltpu.VMEM((count, 2, width, windows), jnp.bfloat16),
                pltpu.VMEM((count, 2, width, group), jnp.float32),
                pltpu.VMEM((count, 2, width, group), jnp.bfloat16),
                pltpu.SemaphoreType.DMA((count * (len(rows) + len(columns) + 1),)),
            ],
        ),
        out_shape=shape,
        input_output_aliases=aliases,
        compiler_params=pltpu.CompilerParams(vmem_limit_bytes=VMEM_BYTES),
        cost_estimate=pl.CostEstimate(flops=1, bytes_accessed=1, transcendentals=0),
        name="cross_" + kind,
    )(place, *operands)


def place_kernel(pairs, place_ref, *refs):
    count = len(pairs)
    came_refs, out_ref = refs[:count], refs[count + 1]
    old_ref, new_ref, sems = refs[count + 2:]
    place = place_ref[0]
    reads = [pltpu.make_async_copy(came_refs[n], old_ref.at[n], sems.at[n]) for n in range(count)]
    for copy in reads:
        copy.start()
    writes = []
    for n, (pair, split) in enumerate(pairs):
        reads[n].wait()
        new_ref[n] = old_ref[n].astype(jnp.float32)
        at = bin_of(place, pair, split, 1)
        writes.append(pltpu.make_async_copy(new_ref.at[n], out_ref.at[at], sems.at[count + n]))
        writes[n].start()
    for copy in writes:
        copy.wait()


def place_blocks(place, pairs, came, out):
    count = len(came)
    return pl.pallas_call(
        functools.partial(place_kernel, pairs),
        grid_spec=pltpu.PrefetchScalarGridSpec(
            num_scalar_prefetch=1,
            grid=(1,),
            in_specs=[pl.BlockSpec(memory_space=pl.ANY)] * (count + 1),
            out_specs=pl.BlockSpec(memory_space=pl.ANY),
            scratch_shapes=[
                pltpu.VMEM((count, *out.shape[1:]), jnp.bfloat16),
                pltpu.VMEM((count, *out.shape[1:]), jnp.float32),
                pltpu.SemaphoreType.DMA((2 * count,)),
            ],
        ),
        out_shape=jax.ShapeDtypeStruct(out.shape, jnp.float32),
        input_output_aliases={count + 1: 0},
        compiler_params=pltpu.CompilerParams(vmem_limit_bytes=VMEM_BYTES),
        cost_estimate=pl.CostEstimate(flops=1, bytes_accessed=1, transcendentals=0),
        name="place",
    )(place, *came, out)


def shards(spectra, valid):
    bins = spectra.shape[0]
    reach = lax.axis_size("rcol") // 2 + 1
    place = lax.axis_index("rrow").astype(jnp.int32)[None]
    held = dict(zip(WHITE, whiten(tuple(WHITE.values()), SPLITS, place, spectra, valid)))

    def move(name):
        if name in TAKEN:
            source, slot = TAKEN[name]
            held[name] = held[source][slot:slot + 1]
            return
        source, axis, step = SENT[name]
        value, gates = held[source], GATES.get(name, ())
        if gates:
            value, *rest = lax.optimization_barrier((value, *(held[gate] for gate in gates)))
            held.update(zip(gates, rest))
        if axis == "came":
            held[name] = moved_by_xor(value, "rrow", step)
            return
        if axis == "rrow":
            held[name] = moved_by_xor(value, axis, step)
            return
        for d in ([step] if step < FAR else range(step, reach)):
            held[name[:-1] + str(d)] = moved_by_shift(value, axis, -d)

    def columns(name, slot):
        return [(held[name], slot)] + [(held[name + "_y" + str(d)], slot) for d in range(1, reach)]

    def job(k, side):
        rows = [(held[name], slot) for name, slot in ROWS[k]]
        return (k, SPLITS[k], rows, columns(*COLUMNS[k][side]))

    out = None
    for name in ORDER:
        if name.startswith("far"):
            k = int(name[3:])
            held[name] = cross(place, "far", [job(k, 1)], None, bins)
        elif name.startswith("near"):
            out = cross(place, "near", [job(int(k), 0) for k in name[4:]], out, bins)
        elif name.startswith("place"):
            pairs = [int(k) for k in name[5:]]
            out = place_blocks(place, [(k, SPLITS[k]) for k in pairs], [held["came" + str(k)] for k in pairs], out)
        else:
            with jax.named_scope(name):
                move(name)
    return jnp.swapaxes(out, 2, 3)


def solution(mesh):
    in_specs = (P("band", None, ("rcol", "rrow"), None), P(("rcol", "rrow"), None))
    out_specs = P("band", None, "rcol", "rrow")
    return jax.shard_map(shards, mesh=mesh, in_specs=in_specs, out_specs=out_specs, check_vma=False)
```

```python
import functools

import jax
import jax.numpy as jnp
from jax import lax
from jax.experimental import pallas as pl
from jax.experimental.pallas import tpu as pltpu
from jax.sharding import PartitionSpec as P

VMEM_BYTES = 32 * 1024 * 1024


def moved_by_xor(value, axis, bits):
    count = lax.axis_size(axis)
    return lax.ppermute(value, axis, [(source, source ^ bits) for source in range(count)])


def moved_by_shift(value, axis, steps):
    count = lax.axis_size(axis)
    return lax.ppermute(value, axis, [(source, (source + steps) % count) for source in range(count)])


SPLITS = (4, 4, 2)
WHITE = {
    "own": ((0, 0), (1, 0), (2, 0)),
    "front": ((0, 0), (1, 0)),
    "back": ((2, 0),),
    "front_other": ((0, 1), (1, 1)),
    "back_other": ((2, 1),),
}
SENT = {
    "got": ("front_other", "rrow", 4),
    "own_x": ("own", "rrow", 1),
    "front_z": ("front", "rrow", 2),
    "own_y1": ("own", "rcol", 1),
    "own_y2": ("own", "rcol", 2),
    "front_d": ("front_z", "rrow", 1),
    "last": ("back_other", "rrow", 2),
    "back_z": ("back", "rrow", 4),
    "got_z": ("got", "rrow", 2),
    "got_x": ("got", "rrow", 1),
    "got_y1": ("got", "rcol", 1),
    "got_y2": ("got", "rcol", 2),
    "got_d": ("got_z", "rrow", 1),
    "last_z": ("last", "rrow", 4),
    "back_d": ("back_z", "rrow", 1),
    "last_x": ("last", "rrow", 1),
    "last_y1": ("last", "rcol", 1),
    "last_y2": ("last", "rcol", 2),
    "last_d": ("last_z", "rrow", 1),
    "came0": ("far0", "came", 4),
    "came1": ("far1", "came", 4),
    "came2": ("far2", "came", 2),
}
TAKEN = {}
ROWS = {
    0: [("own", 0), ("own_x", 0), ("front_z", 0), ("front_d", 0), ("got", 0), ("got_x", 0), ("got_z", 0), ("got_d", 0)],
    1: [("own", 1), ("own_x", 1), ("front_z", 1), ("front_d", 1), ("got", 1), ("got_x", 1), ("got_z", 1), ("got_d", 1)],
    2: [("own", 2), ("own_x", 2), ("last", 0), ("last_x", 0), ("back_z", 0), ("back_d", 0), ("last_z", 0), ("last_d", 0)],
}
COLUMNS = {
    0: (("own", 0), ("got", 0)),
    1: (("own", 1), ("got", 1)),
    2: (("own", 2), ("last", 0)),
}
FAR = 2
ORDER = ("got", "own_x", "front_z", "own_y1", "own_y2", "front_d", "last", "back_z", "got_z", "got_x", "got_y1", "got_y2", "got_d", "last_z", "back_d", "last_x", "last_y1", "last_y2", "last_d", "far0", "came0", "far1", "came1", "far2", "came2", "near012", "place01", "place2")
GATES = {
    "last": ["front_z"],
    "back_z": ["got"],
    "got_z": ["last"],
    "got_x": ["own_x"],
    "got_y1": ["own_y1"],
    "got_y2": ["own_y2"],
    "got_d": ["front_d"],
    "last_z": ["back_z"],
    "back_d": ["got_x"],
    "last_x": ["got_d"],
    "last_y1": ["got_y1"],
    "last_y2": ["got_y2"],
    "last_d": ["back_d"],
}


def bin_of(place, pair, split, other):
    return 2 * pair + ((place // split) % 2 + other) % 2


def whiten_kernel(plan, splits, place_ref, spectra_ref, valid_ref, *out_refs):
    bins = spectra_ref.shape[0]
    total = spectra_ref[0, 0] * spectra_ref[0, 0] + spectra_ref[0, 1] * spectra_ref[0, 1]
    for f in range(1, bins):
        total = total + (spectra_ref[f, 0] * spectra_ref[f, 0] + spectra_ref[f, 1] * spectra_ref[f, 1])
    amplitude = jnp.sqrt(jnp.maximum(total / bins, 1.0))
    factor = valid_ref[...].astype(jnp.float32) / amplitude
    place = place_ref[0]
    for pair, split in enumerate(splits):
        for other in range(2):
            for part in range(2):
                value = (spectra_ref[bin_of(place, pair, split, other), part] * factor).astype(jnp.bfloat16)
                for out_ref, slabs in zip(out_refs, plan):
                    if (pair, other) in slabs:
                        out_ref[slabs.index((pair, other)), part] = value


def whiten(plan, splits, place, spectra, valid):
    bins, _, channels, windows = spectra.shape
    tile = windows // 2 if windows % 256 == 0 else windows
    return pl.pallas_call(
        functools.partial(whiten_kernel, plan, splits),
        grid_spec=pltpu.PrefetchScalarGridSpec(
            num_scalar_prefetch=1,
            grid=(windows // tile,),
            in_specs=[
                pl.BlockSpec((bins, 2, channels, tile), lambda i, p: (0, 0, 0, i)),
                pl.BlockSpec((channels, tile), lambda i, p: (0, i)),
            ],
            out_specs=[pl.BlockSpec((len(slabs), 2, channels, tile), lambda i, p: (0, 0, 0, i)) for slabs in plan],
        ),
        out_shape=[jax.ShapeDtypeStruct((len(slabs), 2, channels, windows), jnp.bfloat16) for slabs in plan],
        compiler_params=pltpu.CompilerParams(vmem_limit_bytes=VMEM_BYTES),
        cost_estimate=pl.CostEstimate(flops=1, bytes_accessed=1, transcendentals=0),
        name="whiten",
    )(place, spectra, valid)


def cross_kernel(jobs, place_ref, *refs):
    left_ref, right_ref, mine_ref, theirs_ref, sems = refs[-5:]
    out_ref = refs[-6]
    place = place_ref[0]
    height, windows = refs[0].shape[2:]
    moves, started = [], []

    def move(source, target):
        copy = pltpu.make_async_copy(source, target, sems.at[len(started)])
        copy.start()
        started.append(copy)
        return copy

    given = iter(refs)
    for n, (_, _, kind, row_slots, column_slots) in enumerate(jobs):
        arriving = []
        for label, slot in enumerate(row_slots):
            start = pl.multiple_of((place ^ label) * height, 16)
            arriving.append(move(next(given).at[slot], left_ref.at[n, :, pl.ds(start, height)]))
        for d, slot in enumerate(column_slots):
            arriving.append(move(next(given).at[slot], right_ref.at[n, :, pl.ds(d * height, height)]))
        moves.append(arriving)

    scale = 1.0 / windows
    leaving = []
    for n, (pair, split, kind, _, _) in enumerate(jobs):
        for copy in moves[n]:
            copy.wait()
        group, width = left_ref.shape[2], right_ref.shape[2]
        right = right_ref[n].reshape(2 * width, windows)
        left = left_ref[n].reshape(2 * group, windows)
        sums = scale * lax.dot_general(right, left, (((1,), (1,)), ((), ())), preferred_element_type=jnp.float32)
        block_ref = mine_ref if kind == "near" else theirs_ref
        block_ref[n, 0] = (sums[:width, :group] + sums[width:, group:]).astype(block_ref.dtype)
        block_ref[n, 1] = (sums[:width, group:] - sums[width:, :group]).astype(block_ref.dtype)
        target = out_ref.at[bin_of(place, pair, split, 0)] if kind == "near" else out_ref
        leaving.append(move(block_ref.at[n], target))
    for copy in leaving:
        copy.wait()


def cross(place, kind, jobs, out, bins):
    count = len(jobs)
    operands = [array for _, _, rows, columns in jobs for array, _ in (*rows, *columns)]
    plan = [
        (pair, split, kind, tuple(slot for _, slot in rows), tuple(slot for _, slot in columns))
        for pair, split, rows, columns in jobs
    ]
    _, _, rows, columns = jobs[0]
    *_, height, windows = operands[0].shape
    group, width = len(rows) * height, len(columns) * height
    aliases = {}
    if out is not None:
        operands.append(out)
        aliases = {len(operands): 0}
    shape = jax.ShapeDtypeStruct((2, width, group), jnp.bfloat16)
    if kind == "near":
        shape = jax.ShapeDtypeStruct((bins, 2, width, group), jnp.float32)
    return pl.pallas_call(
        functools.partial(cross_kernel, plan),
        grid_spec=pltpu.PrefetchScalarGridSpec(
            num_scalar_prefetch=1,
            grid=(1,),
            in_specs=[pl.BlockSpec(memory_space=pl.ANY)] * len(operands),
            out_specs=pl.BlockSpec(memory_space=pl.ANY),
            scratch_shapes=[
                pltpu.VMEM((count, 2, group, windows), jnp.bfloat16),
                pltpu.VMEM((count, 2, width, windows), jnp.bfloat16),
                pltpu.VMEM((count, 2, width, group), jnp.float32),
                pltpu.VMEM((count, 2, width, group), jnp.bfloat16),
                pltpu.SemaphoreType.DMA((count * (len(rows) + len(columns) + 1),)),
            ],
        ),
        out_shape=shape,
        input_output_aliases=aliases,
        compiler_params=pltpu.CompilerParams(vmem_limit_bytes=VMEM_BYTES),
        cost_estimate=pl.CostEstimate(flops=1, bytes_accessed=1, transcendentals=0),
        name="cross_" + kind,
    )(place, *operands)


def place_kernel(pairs, place_ref, *refs):
    count = len(pairs)
    came_refs, out_ref = refs[:count], refs[count + 1]
    old_ref, new_ref, sems = refs[count + 2:]
    place = place_ref[0]
    reads = [pltpu.make_async_copy(came_refs[n], old_ref.at[n], sems.at[n]) for n in range(count)]
    for copy in reads:
        copy.start()
    writes = []
    for n, (pair, split) in enumerate(pairs):
        reads[n].wait()
        new_ref[n] = old_ref[n].astype(jnp.float32)
        at = bin_of(place, pair, split, 1)
        writes.append(pltpu.make_async_copy(new_ref.at[n], out_ref.at[at], sems.at[count + n]))
        writes[n].start()
    for copy in writes:
        copy.wait()


def place_blocks(place, pairs, came, out):
    count = len(came)
    return pl.pallas_call(
        functools.partial(place_kernel, pairs),
        grid_spec=pltpu.PrefetchScalarGridSpec(
            num_scalar_prefetch=1,
            grid=(1,),
            in_specs=[pl.BlockSpec(memory_space=pl.ANY)] * (count + 1),
            out_specs=pl.BlockSpec(memory_space=pl.ANY),
            scratch_shapes=[
                pltpu.VMEM((count, *out.shape[1:]), jnp.bfloat16),
                pltpu.VMEM((count, *out.shape[1:]), jnp.float32),
                pltpu.SemaphoreType.DMA((2 * count,)),
            ],
        ),
        out_shape=jax.ShapeDtypeStruct(out.shape, jnp.float32),
        input_output_aliases={count + 1: 0},
        compiler_params=pltpu.CompilerParams(vmem_limit_bytes=VMEM_BYTES),
        cost_estimate=pl.CostEstimate(flops=1, bytes_accessed=1, transcendentals=0),
        name="place",
    )(place, *came, out)


def shards(spectra, valid):
    bins = spectra.shape[0]
    reach = lax.axis_size("rcol") // 2 + 1
    place = lax.axis_index("rrow").astype(jnp.int32)[None]
    held = dict(zip(WHITE, whiten(tuple(WHITE.values()), SPLITS, place, spectra, valid)))

    def move(name):
        if name in TAKEN:
            source, slot = TAKEN[name]
            held[name] = held[source][slot:slot + 1]
            return
        source, axis, step = SENT[name]
        value, gates = held[source], GATES.get(name, ())
        if gates:
            value, *rest = lax.optimization_barrier((value, *(held[gate] for gate in gates)))
            held.update(zip(gates, rest))
        if axis == "came":
            held[name] = moved_by_xor(value, "rrow", step)
            return
        if axis == "rrow":
            held[name] = moved_by_xor(value, axis, step)
            return
        for d in ([step] if step < FAR else range(step, reach)):
            held[name[:-1] + str(d)] = moved_by_shift(value, axis, -d)

    def columns(name, slot):
        return [(held[name], slot)] + [(held[name + "_y" + str(d)], slot) for d in range(1, reach)]

    def job(k, side):
        rows = [(held[name], slot) for name, slot in ROWS[k]]
        return (k, SPLITS[k], rows, columns(*COLUMNS[k][side]))

    out = None
    for name in ORDER:
        if name.startswith("far"):
            k = int(name[3:])
            held[name] = cross(place, "far", [job(k, 1)], None, bins)
        elif name.startswith("near"):
            out = cross(place, "near", [job(int(k), 0) for k in name[4:]], out, bins)
        elif name.startswith("place"):
            pairs = [int(k) for k in name[5:]]
            out = place_blocks(place, [(k, SPLITS[k]) for k in pairs], [held["came" + str(k)] for k in pairs], out)
        else:
            with jax.named_scope(name):
                move(name)
    return jnp.swapaxes(out, 2, 3)


def solution(mesh):
    in_specs = (P("band", None, ("rcol", "rrow"), None), P(("rcol", "rrow"), None))
    out_specs = P("band", None, "rcol", "rrow")
    return jax.shard_map(shards, mesh=mesh, in_specs=in_specs, out_specs=out_specs, check_vma=False)
```

```python
import functools

import jax
import jax.numpy as jnp
from jax import lax
from jax.experimental import pallas as pl
from jax.experimental.pallas import tpu as pltpu
from jax.sharding import PartitionSpec as P

VMEM_BYTES = 32 * 1024 * 1024


def moved_by_xor(value, axis, bits):
    count = lax.axis_size(axis)
    return lax.ppermute(value, axis, [(source, source ^ bits) for source in range(count)])


def moved_by_shift(value, axis, steps):
    count = lax.axis_size(axis)
    return lax.ppermute(value, axis, [(source, (source + steps) % count) for source in range(count)])


SPLITS = (4, 4, 2)
WHITE = {
    "own": ((0, 0), (1, 0), (2, 0)),
    "front": ((0, 0), (1, 0)),
    "back": ((2, 0),),
    "front_other": ((0, 1), (1, 1)),
    "back_other": ((2, 1),),
}
SENT = {
    "got": ("front_other", "rrow", 4),
    "own_x": ("own", "rrow", 1),
    "front_z": ("front", "rrow", 2),
    "own_y1": ("own", "rcol", 1),
    "own_y2": ("own", "rcol", 2),
    "front_d": ("front_z", "rrow", 1),
    "last": ("back_other", "rrow", 2),
    "back_z": ("back", "rrow", 4),
    "got_z": ("got", "rrow", 2),
    "got_x": ("got", "rrow", 1),
    "got_y1": ("got", "rcol", 1),
    "got_y2": ("got", "rcol", 2),
    "got_d": ("got_z", "rrow", 1),
    "last_z": ("last", "rrow", 4),
    "back_d": ("back_z", "rrow", 1),
    "last_x": ("last", "rrow", 1),
    "last_y1": ("last", "rcol", 1),
    "last_y2": ("last", "rcol", 2),
    "last_d": ("last_z", "rrow", 1),
    "came0": ("far0", "came", 4),
    "came1": ("far1", "came", 4),
    "came2": ("far2", "came", 2),
}
TAKEN = {}
ROWS = {
    0: [("own", 0), ("own_x", 0), ("front_z", 0), ("front_d", 0), ("got", 0), ("got_x", 0), ("got_z", 0), ("got_d", 0)],
    1: [("own", 1), ("own_x", 1), ("front_z", 1), ("front_d", 1), ("got", 1), ("got_x", 1), ("got_z", 1), ("got_d", 1)],
    2: [("own", 2), ("own_x", 2), ("last", 0), ("last_x", 0), ("back_z", 0), ("back_d", 0), ("last_z", 0), ("last_d", 0)],
}
COLUMNS = {
    0: (("own", 0), ("got", 0)),
    1: (("own", 1), ("got", 1)),
    2: (("own", 2), ("last", 0)),
}
FAR = 2
ORDER = ("got", "own_x", "front_z", "own_y1", "own_y2", "front_d", "last", "back_z", "got_z", "got_y1", "got_y2", "got_d", "last_z", "last_y1", "last_y2", "last_x", "got_x", "far1", "came1", "back_d", "last_d", "far0", "came0", "far2", "came2", "near102", "place10", "place2")
GATES = {
    "last": ["own_y2"],
    "back_z": ["got"],
    "got_z": ["last"],
    "got_x": ["own_x"],
    "got_y1": ["own_y1"],
    "got_y2": ["own_y2"],
    "got_d": ["front_d"],
    "last_z": ["back_z"],
    "back_d": ["got_x"],
    "last_x": ["got_d"],
    "last_y1": ["got_y1"],
    "last_y2": ["got_y2"],
    "last_d": ["back_d"],
}


def bin_of(place, pair, split, other):
    return 2 * pair + ((place // split) % 2 + other) % 2


def whiten_kernel(plan, splits, place_ref, spectra_ref, valid_ref, *out_refs):
    bins = spectra_ref.shape[0]
    total = spectra_ref[0, 0] * spectra_ref[0, 0] + spectra_ref[0, 1] * spectra_ref[0, 1]
    for f in range(1, bins):
        total = total + (spectra_ref[f, 0] * spectra_ref[f, 0] + spectra_ref[f, 1] * spectra_ref[f, 1])
    amplitude = jnp.sqrt(jnp.maximum(total / bins, 1.0))
    factor = valid_ref[...].astype(jnp.float32) / amplitude
    place = place_ref[0]
    for pair, split in enumerate(splits):
        for other in range(2):
            for part in range(2):
                value = (spectra_ref[bin_of(place, pair, split, other), part] * factor).astype(jnp.bfloat16)
                for out_ref, slabs in zip(out_refs, plan):
                    if (pair, other) in slabs:
                        out_ref[slabs.index((pair, other)), part] = value


def whiten(plan, splits, place, spectra, valid):
    bins, _, channels, windows = spectra.shape
    tile = windows // 2 if windows % 256 == 0 else windows
    return pl.pallas_call(
        functools.partial(whiten_kernel, plan, splits),
        grid_spec=pltpu.PrefetchScalarGridSpec(
            num_scalar_prefetch=1,
            grid=(windows // tile,),
            in_specs=[
                pl.BlockSpec((bins, 2, channels, tile), lambda i, p: (0, 0, 0, i)),
                pl.BlockSpec((channels, tile), lambda i, p: (0, i)),
            ],
            out_specs=[pl.BlockSpec((len(slabs), 2, channels, tile), lambda i, p: (0, 0, 0, i)) for slabs in plan],
        ),
        out_shape=[jax.ShapeDtypeStruct((len(slabs), 2, channels, windows), jnp.bfloat16) for slabs in plan],
        compiler_params=pltpu.CompilerParams(vmem_limit_bytes=VMEM_BYTES),
        cost_estimate=pl.CostEstimate(flops=1, bytes_accessed=1, transcendentals=0),
        name="whiten",
    )(place, spectra, valid)


def cross_kernel(jobs, place_ref, *refs):
    left_ref, right_ref, mine_ref, theirs_ref, sems = refs[-5:]
    out_ref = refs[-6]
    place = place_ref[0]
    height, windows = refs[0].shape[2:]
    moves, started = [], []

    def move(source, target):
        copy = pltpu.make_async_copy(source, target, sems.at[len(started)])
        copy.start()
        started.append(copy)
        return copy

    given = iter(refs)
    for n, (_, _, kind, row_slots, column_slots) in enumerate(jobs):
        arriving = []
        for label, slot in enumerate(row_slots):
            start = pl.multiple_of((place ^ label) * height, 16)
            arriving.append(move(next(given).at[slot], left_ref.at[n, :, pl.ds(start, height)]))
        for d, slot in enumerate(column_slots):
            arriving.append(move(next(given).at[slot], right_ref.at[n, :, pl.ds(d * height, height)]))
        moves.append(arriving)

    scale = 1.0 / windows
    leaving = []
    for n, (pair, split, kind, _, _) in enumerate(jobs):
        for copy in moves[n]:
            copy.wait()
        group, width = left_ref.shape[2], right_ref.shape[2]
        right = right_ref[n].reshape(2 * width, windows)
        left = left_ref[n].reshape(2 * group, windows)
        sums = scale * lax.dot_general(right, left, (((1,), (1,)), ((), ())), preferred_element_type=jnp.float32)
        block_ref = mine_ref if kind == "near" else theirs_ref
        block_ref[n, 0] = (sums[:width, :group] + sums[width:, group:]).astype(block_ref.dtype)
        block_ref[n, 1] = (sums[:width, group:] - sums[width:, :group]).astype(block_ref.dtype)
        target = out_ref.at[bin_of(place, pair, split, 0)] if kind == "near" else out_ref
        leaving.append(move(block_ref.at[n], target))
    for copy in leaving:
        copy.wait()


def cross(place, kind, jobs, out, bins):
    count = len(jobs)
    operands = [array for _, _, rows, columns in jobs for array, _ in (*rows, *columns)]
    plan = [
        (pair, split, kind, tuple(slot for _, slot in rows), tuple(slot for _, slot in columns))
        for pair, split, rows, columns in jobs
    ]
    _, _, rows, columns = jobs[0]
    *_, height, windows = operands[0].shape
    group, width = len(rows) * height, len(columns) * height
    aliases = {}
    if out is not None:
        operands.append(out)
        aliases = {len(operands): 0}
    shape = jax.ShapeDtypeStruct((2, width, group), jnp.bfloat16)
    if kind == "near":
        shape = jax.ShapeDtypeStruct((bins, 2, width, group), jnp.float32)
    return pl.pallas_call(
        functools.partial(cross_kernel, plan),
        grid_spec=pltpu.PrefetchScalarGridSpec(
            num_scalar_prefetch=1,
            grid=(1,),
            in_specs=[pl.BlockSpec(memory_space=pl.ANY)] * len(operands),
            out_specs=pl.BlockSpec(memory_space=pl.ANY),
            scratch_shapes=[
                pltpu.VMEM((count, 2, group, windows), jnp.bfloat16),
                pltpu.VMEM((count, 2, width, windows), jnp.bfloat16),
                pltpu.VMEM((count, 2, width, group), jnp.float32),
                pltpu.VMEM((count, 2, width, group), jnp.bfloat16),
                pltpu.SemaphoreType.DMA((count * (len(rows) + len(columns) + 1),)),
            ],
        ),
        out_shape=shape,
        input_output_aliases=aliases,
        compiler_params=pltpu.CompilerParams(vmem_limit_bytes=VMEM_BYTES),
        cost_estimate=pl.CostEstimate(flops=1, bytes_accessed=1, transcendentals=0),
        name="cross_" + kind,
    )(place, *operands)


def place_kernel(pairs, place_ref, *refs):
    count = len(pairs)
    came_refs, out_ref = refs[:count], refs[count + 1]
    old_ref, new_ref, sems = refs[count + 2:]
    place = place_ref[0]
    reads = [pltpu.make_async_copy(came_refs[n], old_ref.at[n], sems.at[n]) for n in range(count)]
    for copy in reads:
        copy.start()
    writes = []
    for n, (pair, split) in enumerate(pairs):
        reads[n].wait()
        new_ref[n] = old_ref[n].astype(jnp.float32)
        at = bin_of(place, pair, split, 1)
        writes.append(pltpu.make_async_copy(new_ref.at[n], out_ref.at[at], sems.at[count + n]))
        writes[n].start()
    for copy in writes:
        copy.wait()


def place_blocks(place, pairs, came, out):
    count = len(came)
    return pl.pallas_call(
        functools.partial(place_kernel, pairs),
        grid_spec=pltpu.PrefetchScalarGridSpec(
            num_scalar_prefetch=1,
            grid=(1,),
            in_specs=[pl.BlockSpec(memory_space=pl.ANY)] * (count + 1),
            out_specs=pl.BlockSpec(memory_space=pl.ANY),
            scratch_shapes=[
                pltpu.VMEM((count, *out.shape[1:]), jnp.bfloat16),
                pltpu.VMEM((count, *out.shape[1:]), jnp.float32),
                pltpu.SemaphoreType.DMA((2 * count,)),
            ],
        ),
        out_shape=jax.ShapeDtypeStruct(out.shape, jnp.float32),
        input_output_aliases={count + 1: 0},
        compiler_params=pltpu.CompilerParams(vmem_limit_bytes=VMEM_BYTES),
        cost_estimate=pl.CostEstimate(flops=1, bytes_accessed=1, transcendentals=0),
        name="place",
    )(place, *came, out)


def shards(spectra, valid):
    bins = spectra.shape[0]
    reach = lax.axis_size("rcol") // 2 + 1
    place = lax.axis_index("rrow").astype(jnp.int32)[None]
    held = dict(zip(WHITE, whiten(tuple(WHITE.values()), SPLITS, place, spectra, valid)))

    def move(name):
        if name in TAKEN:
            source, slot = TAKEN[name]
            held[name] = held[source][slot:slot + 1]
            return
        source, axis, step = SENT[name]
        value, gates = held[source], GATES.get(name, ())
        if gates:
            value, *rest = lax.optimization_barrier((value, *(held[gate] for gate in gates)))
            held.update(zip(gates, rest))
        if axis == "came":
            held[name] = moved_by_xor(value, "rrow", step)
            return
        if axis == "rrow":
            held[name] = moved_by_xor(value, axis, step)
            return
        for d in ([step] if step < FAR else range(step, reach)):
            held[name[:-1] + str(d)] = moved_by_shift(value, axis, -d)

    def columns(name, slot):
        return [(held[name], slot)] + [(held[name + "_y" + str(d)], slot) for d in range(1, reach)]

    def job(k, side):
        rows = [(held[name], slot) for name, slot in ROWS[k]]
        return (k, SPLITS[k], rows, columns(*COLUMNS[k][side]))

    out = None
    for name in ORDER:
        if name.startswith("far"):
            k = int(name[3:])
            held[name] = cross(place, "far", [job(k, 1)], None, bins)
        elif name.startswith("near"):
            out = cross(place, "near", [job(int(k), 0) for k in name[4:]], out, bins)
        elif name.startswith("place"):
            pairs = [int(k) for k in name[5:]]
            out = place_blocks(place, [(k, SPLITS[k]) for k in pairs], [held["came" + str(k)] for k in pairs], out)
        else:
            with jax.named_scope(name):
                move(name)
    return jnp.swapaxes(out, 2, 3)


def solution(mesh):
    in_specs = (P("band", None, ("rcol", "rrow"), None), P(("rcol", "rrow"), None))
    out_specs = P("band", None, "rcol", "rrow")
    return jax.shard_map(shards, mesh=mesh, in_specs=in_specs, out_specs=out_specs, check_vma=False)
```
